256 devices in a mesh: row: 8 (over z), col: 32 (over x, y, core).
Axes of the slice: x: 4, y: 4, z: 8, core: 2. Of those that a mesh axis runs over, the one named last changes fastest.
Arguments:
- inputs: bfloat16 [768, 12288], P('col', 'row'), may hold values from -6 to 6
- grad_output: bfloat16 [768, 12288], P('col', 'row'), may hold values from -2 to 2
- up_weight: bfloat16 [12288, 24576], P('row', 'col'), may hold values from -0.0546875 to 0.0546875
- down_weight: bfloat16 [24576, 12288], P('col', 'row'), may hold values from -0.0390625 to 0.0390625
Outputs:
- grad_inputs: bfloat16 [768, 12288], P('col', 'row')
- grad_up: bfloat16 [12288, 24576], P('row', 'col')
- grad_down: bfloat16 [24576, 12288], P('col', 'row')
The draws below stay inside these ranges and needn't reach their ends.
All inputs are finite; a program needn't handle non-finite values.
Results may differ from the reference program's by a relative error of at most 0.005.
Values may be sent and summed in bfloat16 or wider, within the bound.
No kernel may reach another device: no remote copies, remote signals or barrier semaphores. Data moves between devices by JAX's collectives and lax.ppermute only.
A program may use at most 64 MiB of HBM per device.

```python
import jax
import jax.numpy as jnp

D = 12288
FF = 24576
TOKENS = 768


def steps_of(stream_key, extent, split, least, high):
    loudness, own = 1.0, jax.random.fold_in(stream_key, 6)
    for dim, parts in split:
        heights = jnp.exp(jax.random.uniform(jax.random.fold_in(own, dim), (parts,), jnp.float32, least / len(split), high / len(split)))
        loudness = loudness * jnp.repeat(heights, extent[dim] // parts).reshape([-1 if axis == dim else 1 for axis in range(len(extent))])
    return loudness


def scatter_about(stream_key, extent, deviation, most, pieces=(), held_as=jnp.bfloat16):
    level = steps_of(stream_key, extent, pieces, -0.22, 0.18) if pieces else 1.0
    drawn = jax.random.normal(stream_key, extent, jnp.float32) * deviation * level
    return jnp.minimum(jnp.maximum(drawn, -most), most).astype(held_as)


def setup_inputs(seed: int = 0) -> dict:
    splits = jax.random.split(jax.random.key(seed), 5)
    inputs = scatter_about(splits[0], (TOKENS, D), 1.0, 6.0, ((0, 32), (1, 8)))
    grad_output = scatter_about(splits[1], (TOKENS, D), 0.3, 2.0, ((0, 32), (1, 8)))
    up_weight = scatter_about(splits[2], (D, FF), D ** -0.5, 0.0546875, ((0, 8), (1, 32)))
    down_weight = scatter_about(splits[3], (FF, D), FF ** -0.5, 0.0390625, ((0, 32), (1, 8)))
    return dict(inputs=inputs, grad_output=grad_output, up_weight=up_weight, down_weight=down_weight)


def gelu_parts(pre, grad_act):
    act, pull = jax.vjp(lambda value: jax.nn.gelu(value, approximate=True), pre)
    return (act.astype(jnp.bfloat16), pull(grad_act)[0].astype(jnp.bfloat16))

def reference(inputs, grad_output, up_weight, down_weight):
    pre = jnp.dot(inputs, up_weight, preferred_element_type=jnp.float32)
    grad_act = jnp.dot(grad_output, down_weight.T, preferred_element_type=jnp.float32)
    act, grad_pre = gelu_parts(pre, grad_act)
    grad_up = jnp.dot(inputs.T, grad_pre, preferred_element_type=jnp.float32).astype(jnp.bfloat16)
    grad_down = jnp.dot(act.T, grad_output, preferred_element_type=jnp.float32).astype(jnp.bfloat16)
    grad_inputs = jnp.dot(grad_pre, up_weight.T, preferred_element_type=jnp.float32).astype(jnp.bfloat16)
    return (grad_inputs, grad_up, grad_down)
```

```python
import jax
import jax.numpy as jnp
from jax import lax
from jax.sharding import PartitionSpec as P

PRE_SCALE = 32.0
GRAD_SCALE = 128.0
SENT = jnp.float16


def gelu_parts(pre, grad_act):
    act, pull = jax.vjp(lambda value: jax.nn.gelu(value, approximate=True), pre)
    return (act.astype(jnp.bfloat16), pull(grad_act)[0].astype(jnp.bfloat16))


def contract_first(left, right):
    return lax.dot_general(
        left, right, (((0,), (0,)), ((), ())), preferred_element_type=jnp.float32
    )


def contract_last(left, right):
    return lax.dot_general(
        left, right, (((1,), (1,)), ((), ())), preferred_element_type=jnp.float32
    )


def col_pairs(dx, dy, dc):
    pairs = []
    for x in range(4):
        for y in range(4):
            for c in range(2):
                there = (((x + dx) % 4) * 4 + (y + dy) % 4) * 2 + (c + dc) % 2
                pairs.append(((x * 4 + y) * 2 + c, there))
    return pairs


def move_col(value, dx=0, dy=0, dc=0):
    return lax.ppermute(value, "col", col_pairs(dx, dy, dc))


def move_row(value, step):
    return lax.ppermute(value, "row", [(i, (i + step) % 8) for i in range(8)])


def gather_chips(own):
    line = jnp.concatenate(
        [own] + [move_col(own, dx=step) for step in (1, -1, 2)], axis=0
    )
    return [line] + [move_col(line, dy=step) for step in (1, -1, 2)]


def place(pieces, at_row):
    rows, width = pieces[0].shape
    whole = jnp.zeros((8 * rows, width), pieces[0].dtype)
    for j, piece in enumerate(pieces):
        start = lax.rem(j + 8 - at_row, 8) * rows
        whole = lax.dynamic_update_slice(whole, piece, (start, 0))
    return whole


def gather_tokens(own, at_row):
    near = gather_chips(own)
    far = [move_col(piece, dc=1) for piece in near]
    return place(near + far, at_row)


def reduce_rows(partial, right_hops):
    rows = partial.shape[0] // 8
    total = partial[:rows]
    for step, hops in ((1, right_hops), (-1, 7 - right_hops)):
        running = None
        for k in range(hops, 0, -1):
            b = (step * k) % 8
            term = partial[b * rows : (b + 1) * rows]
            running = term if running is None else running + term
            running = move_row(running.astype(SENT), step).astype(jnp.float32)
        total = total + running
    return total


def gather_rows(own, right_hops):
    blocks = {0: own}
    for step, hops in ((1, right_hops), (-1, 7 - right_hops)):
        moving = own
        for k in range(1, hops + 1):
            moving = move_row(moving, step)
            blocks[(-step * k) % 8] = moving
    return jnp.concatenate([blocks[b] for b in range(8)], axis=0)


def scatter_tokens(partial, at_row):
    rows = partial.shape[0] // 8

    def piece(j):
        start = lax.rem(j + 8 - at_row, 8) * rows
        return lax.dynamic_slice(partial, (start, 0), (rows, partial.shape[1]))

    pieces = [
        piece(j) + move_col(piece(j + 4).astype(jnp.bfloat16), dc=1).astype(jnp.float32)
        for j in range(4)
    ]
    line = pieces[0]
    for j, step in ((1, -1), (2, 1), (3, 2)):
        line = line + move_col(pieces[j].astype(jnp.bfloat16), dy=step).astype(jnp.float32)
    rows = rows // 4
    own = line[:rows]
    for j, step in ((1, -1), (2, 1), (3, 2)):
        part = line[j * rows : (j + 1) * rows].astype(jnp.bfloat16)
        own = own + move_col(part, dx=step).astype(jnp.float32)
    return own


def on_device(inputs, grad_output, up_weight, down_weight):
    at_row = lax.axis_index("row")
    all_inputs = gather_tokens(inputs, at_row)
    part_pre = jnp.dot(all_inputs, up_weight, preferred_element_type=jnp.float32)
    pre = reduce_rows(part_pre * PRE_SCALE, 4) * (1 / PRE_SCALE)
    all_grads = gather_tokens(grad_output, at_row)
    part_grad = contract_last(all_grads, down_weight)
    grad_act = reduce_rows(part_grad * GRAD_SCALE, 3) * (1 / GRAD_SCALE)
    act_own, grad_pre_own = gelu_parts(pre, grad_act)
    grad_pre = gather_rows(grad_pre_own, 4)
    act = gather_rows(act_own, 3)
    grad_inputs = scatter_tokens(contract_last(grad_pre, up_weight), at_row)
    grad_up = contract_first(all_inputs, grad_pre).astype(jnp.bfloat16)
    grad_down = contract_first(act, all_grads).astype(jnp.bfloat16)
    return (grad_inputs.astype(jnp.bfloat16), grad_up, grad_down)


def solution(mesh):
    in_specs = (P("col", "row"), P("col", "row"), P("row", "col"), P("col", "row"))
    out_specs = (P("col", "row"), P("row", "col"), P("col", "row"))
    return jax.shard_map(
        on_device, mesh=mesh, in_specs=in_specs, out_specs=out_specs, check_vma=False
    )
```

```python
import jax
import jax.numpy as jnp
from jax import lax
from jax.experimental import pallas as pl
from jax.experimental.pallas import tpu as pltpu
from jax.sharding import PartitionSpec as P

PRE_SCALE = 32.0
GRAD_SCALE = 128.0
SENT = jnp.float16


def gelu_parts(pre, grad_act):
    act, pull = jax.vjp(lambda value: jax.nn.gelu(value, approximate=True), pre)
    return (act.astype(jnp.bfloat16), pull(grad_act)[0].astype(jnp.bfloat16))


def contract_first(left, right):
    return lax.dot_general(
        left, right, (((0,), (0,)), ((), ())), preferred_element_type=jnp.float32
    )


def contract_last(left, right):
    return lax.dot_general(
        left, right, (((1,), (1,)), ((), ())), preferred_element_type=jnp.float32
    )


ALONG = (1, -1, 2)


def col_pairs(to):
    pairs = []
    for x in range(4):
        for y in range(4):
            for c in range(2):
                tx, ty, tc = to(x, y, c)
                there = ((tx % 4) * 4 + ty % 4) * 2 + tc
                pairs.append(((x * 4 + y) * 2 + c, there))
    return pairs


def swap(value):
    return lax.ppermute(value, "col", col_pairs(lambda x, y, c: (x, y, 1 - c)))


def move(value, axis_of_core, step):
    def to(x, y, c):
        return (x + step, y, c) if axis_of_core[c] == "x" else (x, y + step, c)

    return lax.ppermute(value, "col", col_pairs(to))


def move_row(value, step):
    return lax.ppermute(value, "row", [(i, (i + step) % 8) for i in range(8)])


def nothing(*refs):
    pass


def behind(value, *earlier):
    anywhere = pl.BlockSpec(memory_space=pl.ANY)
    return pl.pallas_call(
        nothing,
        out_shape=jax.ShapeDtypeStruct(value.shape, value.dtype),
        in_specs=[anywhere] * (1 + len(earlier)),
        out_specs=anywhere,
        input_output_aliases={0: 0},
        compiler_params=pltpu.CompilerParams(vmem_limit_bytes=128 * 1024),
        cost_estimate=pl.CostEstimate(flops=0, bytes_accessed=0, transcendentals=0),
    )(value, *earlier)


def gather_tokens(pair):
    line = jnp.concatenate([pair] + [move(pair, "xy", step) for step in ALONG], axis=0)
    return [line] + [move(line, "yx", step) for step in ALONG]


def block_start(index, first_core):
    index = lax.rem(index + 8, 8)
    y, x = index // 4 * 2, index // 2 % 2 * 2
    zero = jnp.zeros_like(index)
    return (jnp.where(first_core, y, x), jnp.where(first_core, x, y), index % 2, zero, zero)


def block_of(value, index, first_core):
    rows, width = value.shape[3:]
    start = block_start(index, first_core)
    return lax.dynamic_slice(value, start, (2, 2, 1, rows, width)).reshape(4 * rows, width)


def reduce_rows(first, second, at_row, first_core, meanwhile):
    arrays, hops = (first, second), ({-1: 4, 1: 3}, {1: 4, -1: 3})
    running, sent, last = ({}, {}), second, None
    for s in range(4):
        for a in range(2):
            for step in hops[a]:
                left = hops[a][step] - s
                if left < 1:
                    continue
                term = block_of(arrays[a], at_row + step * left, first_core)
                if s:
                    term = running[a][step] + term
                sent = behind(term, sent, *(meanwhile if s == 1 and sent is last else ()))
                last = last if s else sent
                running[a][step] = move_row(sent.astype(SENT), step).astype(jnp.float32)
    return tuple(
        block_of(arrays[a], at_row, first_core) + running[a][1] + running[a][-1]
        for a in range(2)
    )


def turned(value):
    rows, width = value.shape
    square = value.reshape(2, 2, rows // 4, width)
    return jnp.swapaxes(square, 0, 1).reshape(rows, width)


def gather_rows(first, second, at_row):
    rows, width = first.shape
    hops = ({1: 4, -1: 3}, {-1: 4, 1: 3})

    def put(whole, block, index, a):
        start = block_start(index, True)[:4] + (a * width,)
        return lax.dynamic_update_slice(whole, block.reshape(2, 2, 1, rows // 4, width), start)

    whole = jnp.zeros((4, 4, 2, rows // 4, 2 * width), first.dtype)
    whole = put(put(whole, first, at_row, 0), second, at_row, 1)
    moving, sent = ({1: first, -1: first}, {1: second, -1: second}), None
    for s in range(4):
        for a in range(2):
            for step in hops[a]:
                if hops[a][step] > s:
                    if s:
                        sent = behind(moving[a][step], sent)
                        whole = put(whole, sent, at_row - step * s, a)
                    else:
                        sent = moving[a][step]
                    moving[a][step] = move_row(sent, step)
    for a in range(2):
        for step, last in hops[a].items():
            whole = put(whole, moving[a][step], at_row - step * last, a)
    return whole


def scatter_tokens(kept, given, core, first_core, between):
    tokens, width = kept.shape
    rows = tokens // 16
    half = kept + swap(given).astype(jnp.float32)
    blocks = half.reshape(4, 4, rows, width)
    blocks = jnp.where(first_core, blocks, jnp.swapaxes(blocks, 0, 1))
    line = blocks[0]
    for q, step in ((3, 2), (1, -1), (2, 1)):
        part = blocks[q].reshape(4 * rows, width).astype(jnp.bfloat16)
        part = move(part, "yx", step).astype(jnp.float32)
        line = line + part.reshape(4, rows, width)
    line = behind(line, *between)
    own = line[0]
    for p, step in ((3, 2), (1, -1), (2, 1)):
        part = move(line[p].astype(jnp.bfloat16), "xy", step)
        own = own + part.astype(jnp.float32)
    own = own.astype(jnp.bfloat16)
    rows = rows // 2
    mine = lax.dynamic_slice(own, (core * rows, 0), (rows, width))
    theirs = swap(lax.dynamic_slice(own, ((1 - core) * rows, 0), (rows, width)))
    return jnp.where(
        first_core,
        jnp.concatenate([mine, theirs], axis=1),
        jnp.concatenate([theirs, mine], axis=1),
    )


def on_device(inputs, grad_output, up_weight, down_weight):
    at_row = lax.axis_index("row")
    core = lax.rem(lax.axis_index("col"), 2)
    first_core = core == 0
    tokens, width = 32 * inputs.shape[0], inputs.shape[1]

    here = jnp.where(first_core, inputs, grad_output)
    there = swap(jnp.where(first_core, grad_output, inputs))
    pair = jnp.where(
        first_core,
        jnp.concatenate([here, there], axis=0),
        jnp.concatenate([there, here], axis=0),
    )
    pieces = gather_tokens(pair)

    scales = jnp.array([PRE_SCALE, GRAD_SCALE], jnp.float32).astype(jnp.bfloat16)
    scales = behind(jnp.broadcast_to(scales[:, None], (2, 128)), pieces[0])
    up, down = up_weight * scales[0, 0], down_weight.T * scales[1, 0]
    other_weight = swap(jnp.where(first_core, down, up))
    own_weight = jnp.where(first_core, up, down)
    units = up.shape[1]

    def project(weight):
        parts = [jnp.dot(p, weight, preferred_element_type=jnp.float32) for p in pieces]
        return jnp.stack(parts).reshape(4, 4, 2, inputs.shape[0], units)

    others = [swap(piece) for piece in pieces]
    own_sum, from_other = reduce_rows(
        project(own_weight), project(other_weight), at_row, first_core, others
    )
    from_other = swap(from_other)
    pre = jnp.where(first_core, own_sum, from_other) * (1 / PRE_SCALE)
    grad_act = turned(jnp.where(first_core, from_other, own_sum)) * (1 / GRAD_SCALE)
    act_own, grad_pre_own = gelu_parts(pre, grad_act)

    whole = gather_rows(grad_pre_own, act_own, at_row)
    grad_pre = whole[..., :units].reshape(tokens, units)
    act = jnp.swapaxes(whole[..., units:], 0, 1).reshape(tokens, units)

    def chosen(first, second):
        parts = [jnp.where(first_core, p, o) for p, o in zip(first, second)]
        return jnp.concatenate(parts, axis=0)

    all_inputs, all_grads = chosen(pieces, others), chosen(others, pieces)

    half = width // 2
    give_weight = lax.dynamic_slice_in_dim(up_weight, (1 - core) * half, half, 0)
    keep_weight = lax.dynamic_slice_in_dim(up_weight, core * half, half, 0)
    given = contract_last(grad_pre, give_weight).astype(jnp.bfloat16)
    kept = contract_last(grad_pre, keep_weight)
    kept = lax.optimization_barrier(kept)
    grad_up = contract_first(all_inputs, grad_pre).astype(jnp.bfloat16)
    grad_down = contract_first(act, all_grads).astype(jnp.bfloat16)
    grad_inputs = scatter_tokens(kept, given, core, first_core, (grad_up, grad_down))
    return (grad_inputs, grad_up, grad_down)


def solution(mesh):
    in_specs = (P("col", "row"), P("col", "row"), P("row", "col"), P("col", "row"))
    out_specs = (P("col", "row"), P("row", "col"), P("col", "row"))
    return jax.shard_map(
        on_device, mesh=mesh, in_specs=in_specs, out_specs=out_specs, check_vma=False
    )
```

```python
import jax
import jax.numpy as jnp
from jax import lax
from jax.experimental import pallas as pl
from jax.experimental.pallas import tpu as pltpu
from jax.sharding import PartitionSpec as P

PRE_SCALE = 32.0
GRAD_SCALE = 128.0
SENT = jnp.float16


def gelu_parts(pre, grad_act):
    act, pull = jax.vjp(lambda value: jax.nn.gelu(value, approximate=True), pre)
    return (act.astype(jnp.bfloat16), pull(grad_act)[0].astype(jnp.bfloat16))


def contract_first(left, right):
    return lax.dot_general(
        left, right, (((0,), (0,)), ((), ())), preferred_element_type=jnp.float32
    )


def contract_last(left, right):
    return lax.dot_general(
        left, right, (((1,), (1,)), ((), ())), preferred_element_type=jnp.float32
    )


ALONG = (1, -1, 2)


def col_pairs(to):
    pairs = []
    for x in range(4):
        for y in range(4):
            for c in range(2):
                tx, ty, tc = to(x, y, c)
                there = ((tx % 4) * 4 + ty % 4) * 2 + tc
                pairs.append(((x * 4 + y) * 2 + c, there))
    return pairs


def swap(value):
    return lax.ppermute(value, "col", col_pairs(lambda x, y, c: (x, y, 1 - c)))


def move(value, axis_of_core, step):
    def to(x, y, c):
        return (x + step, y, c) if axis_of_core[c] == "x" else (x, y + step, c)

    return lax.ppermute(value, "col", col_pairs(to))


def move_row(value, step):
    return lax.ppermute(value, "row", [(i, (i + step) % 8) for i in range(8)])


def nothing(*refs):
    pass


def behind(value, *earlier):
    anywhere = pl.BlockSpec(memory_space=pl.ANY)
    return pl.pallas_call(
        nothing,
        out_shape=jax.ShapeDtypeStruct(value.shape, value.dtype),
        in_specs=[anywhere] * (1 + len(earlier)),
        out_specs=anywhere,
        input_output_aliases={0: 0},
        compiler_params=pltpu.CompilerParams(vmem_limit_bytes=128 * 1024),
        cost_estimate=pl.CostEstimate(flops=0, bytes_accessed=0, transcendentals=0),
    )(value, *earlier)


def gather_tokens(pair):
    line = jnp.concatenate([pair] + [move(pair, "xy", step) for step in ALONG], axis=0)
    return [line] + [move(line, "yx", step) for step in ALONG]


def block_start(index, turned):
    index = lax.rem(index + 8, 8)
    y, x = index // 4 * 2, index // 2 % 2 * 2
    zero = jnp.zeros_like(index)
    first, second = jnp.where(turned, x, y), jnp.where(turned, y, x)
    return first, second, index % 2, zero, zero


def block_of(value, index, turned):
    rows, width = value.shape[3:]
    start = block_start(index, turned)
    return lax.dynamic_slice(value, start, (2, 2, 1, rows, width)).reshape(4 * rows, width)


def reduce_rows(first, second, at_row, turned):
    arrays, hops = (first, second), ({-1: 4, 1: 3}, {1: 4, -1: 3})
    running, sent = ({}, {}), second
    for s in range(4):
        for a in range(2):
            for step in hops[a]:
                left = hops[a][step] - s
                if left < 1:
                    continue
                term = block_of(arrays[a], at_row + step * left, turned[a])
                if s:
                    term = running[a][step] + term
                sent = behind(term, sent)
                running[a][step] = move_row(sent.astype(SENT), step).astype(jnp.float32)
    return tuple(
        block_of(arrays[a], at_row, turned[a]) + running[a][1] + running[a][-1]
        for a in range(2)
    )


def turn(value):
    rows, width = value.shape
    square = value.reshape(2, 2, rows // 4, width)
    return jnp.swapaxes(square, 0, 1).reshape(rows, width)


def gather_rows(first, second, at_row):
    rows, width = first.shape
    hops = ({1: 4, -1: 3}, {-1: 4, 1: 3})

    def put(whole, block, index, a):
        start = block_start(index, False)[:4] + (a * width,)
        return lax.dynamic_update_slice(whole, block.reshape(2, 2, 1, rows // 4, width), start)

    whole = jnp.zeros((4, 4, 2, rows // 4, 2 * width), first.dtype)
    whole = put(put(whole, first, at_row, 0), second, at_row, 1)
    moving, sent = ({1: first, -1: first}, {1: second, -1: second}), None
    for s in range(4):
        for a in range(2):
            for step in hops[a]:
                if hops[a][step] > s:
                    if s:
                        sent = behind(moving[a][step], sent)
                        whole = put(whole, sent, at_row - step * s, a)
                    else:
                        sent = moving[a][step]
                    moving[a][step] = move_row(sent, step)
    for a in range(2):
        for step, last in hops[a].items():
            whole = put(whole, moving[a][step], at_row - step * last, a)
    return whole


def scatter_tokens(grad_pre, keep_weight, give_weight, core, meanwhile):
    first_core = core == 0
    straight = grad_pre.reshape(4, -1, grad_pre.shape[1])
    turned = grad_pre.reshape(4, 4, -1, grad_pre.shape[1])
    turned = jnp.swapaxes(turned, 0, 1).reshape(straight.shape)
    mine = jnp.where(first_core, straight, turned)
    theirs = jnp.where(first_core, turned, straight)
    parts, sent = {}, None
    for q in (3, 1, 2, 0):
        given = swap(contract_last(theirs[q], give_weight).astype(jnp.bfloat16))
        parts[q] = contract_last(mine[q], keep_weight) + given.astype(jnp.float32)
    line = parts[0]
    for q, step in ((3, 2), (1, -1), (2, 1)):
        part = parts[q].astype(jnp.bfloat16)
        sent = part if sent is None else behind(part, sent)
        line = line + move(sent, "yx", step).astype(jnp.float32)
    done = meanwhile(sent)
    line = behind(line, *done).reshape(4, -1, line.shape[1])
    own = line[0]
    for p, step in ((3, 2), (1, -1), (2, 1)):
        part = move(line[p].astype(jnp.bfloat16), "xy", step)
        own = own + part.astype(jnp.float32)
    own = own.astype(jnp.bfloat16)
    rows, width = own.shape[0] // 2, own.shape[1]
    kept = lax.dynamic_slice(own, (core * rows, 0), (rows, width))
    other = swap(lax.dynamic_slice(own, ((1 - core) * rows, 0), (rows, width)))
    whole = jnp.where(
        first_core,
        jnp.concatenate([kept, other], axis=1),
        jnp.concatenate([other, kept], axis=1),
    )
    return whole, done


def on_device(inputs, grad_output, up_weight, down_weight):
    at_row = lax.axis_index("row")
    core = lax.rem(lax.axis_index("col"), 2)
    first_core = core == 0
    tokens, width = 32 * inputs.shape[0], inputs.shape[1]

    here = jnp.where(first_core, inputs, grad_output)
    there = swap(jnp.where(first_core, grad_output, inputs))
    pair = jnp.where(
        first_core,
        jnp.concatenate([here, there], axis=0),
        jnp.concatenate([there, here], axis=0),
    )
    pieces = gather_tokens(pair)

    scales = jnp.array([PRE_SCALE, GRAD_SCALE], jnp.float32).astype(jnp.bfloat16)
    scales = behind(jnp.broadcast_to(scales[:, None], (2, 128)), pieces[0])
    up, down = up_weight * scales[0, 0], down_weight.T * scales[1, 0]
    weights = jnp.where(first_core, up, down), jnp.where(first_core, down, up)
    units = up.shape[1]
    sums, others, earlier = ([], []), [], []
    for q in range(4):
        if q:
            pieces[q] = behind(pieces[q], *earlier)
        others.append(swap(pieces[q]))
        for a, piece in enumerate((pieces[q], others[q])):
            sums[a].append(jnp.dot(piece, weights[a], preferred_element_type=jnp.float32))
        earlier = [sums[0][0], sums[1][0]] if q == 0 else [pieces[q]]

    def stacked(parts):
        return jnp.stack(parts).reshape(4, 4, 2, inputs.shape[0], units)

    second_core = jnp.logical_not(first_core)
    own, other = reduce_rows(
        stacked(sums[0]), stacked(sums[1]), at_row, (second_core, first_core)
    )
    pre, grad_act = jnp.where(first_core, own, other), jnp.where(first_core, other, own)
    act_own, grad_pre_own = gelu_parts(
        pre * (1 / PRE_SCALE), turn(grad_act) * (1 / GRAD_SCALE)
    )

    whole = gather_rows(grad_pre_own, act_own, at_row)
    grad_pre = whole[..., :units].reshape(tokens, units)
    act = jnp.swapaxes(whole[..., units:], 0, 1).reshape(tokens, units)

    near = [jnp.where(first_core, p, o) for p, o in zip(pieces, others)]
    far = [jnp.where(first_core, o, p) for p, o in zip(pieces, others)]
    all_inputs, all_grads = jnp.concatenate(near, axis=0), jnp.concatenate(far, axis=0)

    def weight_gradients(sent):
        grad_up = contract_first(behind(all_inputs, sent), grad_pre)
        grad_down = contract_first(act, behind(all_grads, sent))
        return grad_up.astype(jnp.bfloat16), grad_down.astype(jnp.bfloat16)

    half = width // 2
    give_weight = lax.dynamic_slice_in_dim(up_weight, (1 - core) * half, half, 0)
    keep_weight = lax.dynamic_slice_in_dim(up_weight, core * half, half, 0)
    grad_inputs, (grad_up, grad_down) = scatter_tokens(
        grad_pre, keep_weight, give_weight, core, weight_gradients
    )
    return (grad_inputs, grad_up, grad_down)


def solution(mesh):
    in_specs = (P("col", "row"), P("col", "row"), P("row", "col"), P("col", "row"))
    out_specs = (P("col", "row"), P("row", "col"), P("col", "row"))
    return jax.shard_map(
        on_device, mesh=mesh, in_specs=in_specs, out_specs=out_specs, check_vma=False
    )
```

```python
import jax
import jax.numpy as jnp
from jax import lax
from jax.experimental import pallas as pl
from jax.experimental.pallas import tpu as pltpu
from jax.sharding import PartitionSpec as P

PRE_SCALE = 32.0
GRAD_SCALE = 128.0
SENT = jnp.float16


def gelu_parts(pre, grad_act):
    act, pull = jax.vjp(lambda value: jax.nn.gelu(value, approximate=True), pre)
    return (act.astype(jnp.bfloat16), pull(grad_act)[0].astype(jnp.bfloat16))


def contract_first(left, right):
    return lax.dot_general(
        left, right, (((0,), (0,)), ((), ())), preferred_element_type=jnp.float32
    )


def contract_last(left, right):
    return lax.dot_general(
        left, right, (((1,), (1,)), ((), ())), preferred_element_type=jnp.float32
    )


ALONG = (1, -1, 2)


def col_pairs(to):
    pairs = []
    for x in range(4):
        for y in range(4):
            for c in range(2):
                tx, ty, tc = to(x, y, c)
                there = ((tx % 4) * 4 + ty % 4) * 2 + tc
                pairs.append(((x * 4 + y) * 2 + c, there))
    return pairs


def swap(value):
    return lax.ppermute(value, "col", col_pairs(lambda x, y, c: (x, y, 1 - c)))


def move(value, axis_of_core, step):
    def to(x, y, c):
        return (x + step, y, c) if axis_of_core[c] == "x" else (x, y + step, c)

    return lax.ppermute(value, "col", col_pairs(to))


def move_row(value, step):
    return lax.ppermute(value, "row", [(i, (i + step) % 8) for i in range(8)])


def nothing(*refs):
    pass


def behind(value, *earlier):
    anywhere = pl.BlockSpec(memory_space=pl.ANY)
    return pl.pallas_call(
        nothing,
        out_shape=jax.ShapeDtypeStruct(value.shape, value.dtype),
        in_specs=[anywhere] * (1 + len(earlier)),
        out_specs=anywhere,
        input_output_aliases={0: 0},
        compiler_params=pltpu.CompilerParams(vmem_limit_bytes=128 * 1024),
        cost_estimate=pl.CostEstimate(flops=0, bytes_accessed=0, transcendentals=0),
    )(value, *earlier)


def gather_tokens(pair):
    line = jnp.concatenate([pair] + [move(pair, "xy", step) for step in ALONG], axis=0)
    return [line] + [move(line, "yx", step) for step in ALONG]


def block_start(index, turned):
    index = lax.rem(index + 8, 8)
    y, x = index // 4 * 2, index // 2 % 2 * 2
    zero = jnp.zeros_like(index)
    first, second = jnp.where(turned, x, y), jnp.where(turned, y, x)
    return first, second, index % 2, zero, zero


def block_of(value, index, turned):
    rows, width = value.shape[3:]
    start = block_start(index, turned)
    return lax.dynamic_slice(value, start, (2, 2, 1, rows, width)).reshape(4 * rows, width)


def reduce_rows(first, second, at_row, turned):
    arrays, hops = (first, second), ({-1: 4, 1: 3}, {1: 4, -1: 3})
    running, sent = ({}, {}), second
    for s in range(4):
        for hop_count in (4, 3):
            for a in range(2):
                step = next(d for d in hops[a] if hops[a][d] == hop_count)
                left = hop_count - s
                if left < 1:
                    continue
                term = block_of(arrays[a], at_row + step * left, turned[a])
                if s:
                    term = running[a][step] + term
                sent = behind(term, sent)
                running[a][step] = move_row(sent.astype(SENT), step).astype(jnp.float32)
    return tuple(
        block_of(arrays[a], at_row, turned[a]) + running[a][1] + running[a][-1]
        for a in range(2)
    )


def turn(value):
    rows, width = value.shape
    square = value.reshape(2, 2, rows // 4, width)
    return jnp.swapaxes(square, 0, 1).reshape(rows, width)


def gather_rows(first, second, at_row, ready):
    rows, width = first.shape
    hops = ({1: 4, -1: 3}, {-1: 4, 1: 3})

    def put(whole, block, index):
        start = block_start(index, False)
        return lax.dynamic_update_slice(whole, block.reshape(2, 2, 1, rows // 4, width), start)

    empty = jnp.zeros((4, 4, 2, rows // 4, width), first.dtype)
    whole = [put(empty, first, at_row), put(empty, second, at_row)]
    moving, sent = ({1: first, -1: first}, {1: second, -1: second}), None
    for s in range(4):
        for a in range(2):
            for step in hops[a]:
                if s >= hops[a][step]:
                    continue
                if s:
                    sent = behind(moving[a][step], sent, *ready)
                    ready = ()
                    whole[a] = put(whole[a], sent, at_row - step * s)
                else:
                    sent = moving[a][step]
                moving[a][step] = move_row(sent, step)
    for a in range(2):
        for step, last in hops[a].items():
            whole[a] = put(whole[a], moving[a][step], at_row - step * last)
    return whole


def scatter_tokens(grad_pre, keep_weight, give_weight, core, meanwhile):
    first_core = core == 0
    straight = grad_pre.reshape(4, -1, grad_pre.shape[1])
    turned = grad_pre.reshape(4, 4, -1, grad_pre.shape[1])
    turned = jnp.swapaxes(turned, 0, 1).reshape(straight.shape)
    mine = jnp.where(first_core, straight, turned)
    theirs = jnp.where(first_core, turned, straight)
    parts, sent = {}, None
    given = None
    for q in (3, 1, 2, 0):
        rows = theirs[q] if given is None else behind(theirs[q], given)
        given = (contract_last(rows, give_weight) * (1 / PRE_SCALE)).astype(jnp.bfloat16)
        kept = contract_last(mine[q], keep_weight) * (1 / PRE_SCALE)
        parts[q] = kept + swap(given).astype(jnp.float32)
    line = parts[0]
    for q, step in ((3, 2), (1, -1), (2, 1)):
        part = parts[q].astype(jnp.bfloat16)
        sent = part if sent is None else behind(part, sent)
        line = line + move(sent, "yx", step).astype(jnp.float32)
    done = meanwhile(sent)
    line = behind(line, *done).reshape(4, -1, line.shape[1])
    own = line[0]
    for p, step in ((3, 2), (1, -1), (2, 1)):
        part = move(line[p].astype(jnp.bfloat16), "xy", step)
        own = own + part.astype(jnp.float32)
    own = own.astype(jnp.bfloat16)
    rows, width = own.shape[0] // 2, own.shape[1]
    kept = lax.dynamic_slice(own, (core * rows, 0), (rows, width))
    other = swap(lax.dynamic_slice(own, ((1 - core) * rows, 0), (rows, width)))
    whole = jnp.where(
        first_core,
        jnp.concatenate([kept, other], axis=1),
        jnp.concatenate([other, kept], axis=1),
    )
    return whole, done


def on_device(inputs, grad_output, up_weight, down_weight):
    at_row = lax.axis_index("row")
    core = lax.rem(lax.axis_index("col"), 2)
    first_core = core == 0
    tokens, width = 32 * inputs.shape[0], inputs.shape[1]

    here = jnp.where(first_core, inputs, grad_output)
    there = swap(jnp.where(first_core, grad_output, inputs))
    pair = jnp.where(
        first_core,
        jnp.concatenate([here, there], axis=0),
        jnp.concatenate([there, here], axis=0),
    )
    pieces = gather_tokens(pair)

    scales = jnp.array([PRE_SCALE, GRAD_SCALE], jnp.float32).astype(jnp.bfloat16)
    scales = behind(jnp.broadcast_to(scales[:, None], (2, 128)), pieces[0])
    up, down = up_weight * scales[0, 0], down_weight.T * scales[1, 0]
    weights = jnp.where(first_core, up, down), jnp.where(first_core, down, up)
    units = up.shape[1]
    sums, others, earlier = ([None] * 4, [None] * 4), [None] * 4, []
    for q in (0, 3, 1, 2):
        if q:
            pieces[q] = behind(pieces[q], *earlier)
        others[q] = swap(pieces[q])
        for a, piece in enumerate((pieces[q], others[q])):
            sums[a][q] = jnp.dot(piece, weights[a], preferred_element_type=jnp.float32)
        earlier = [pieces[1]] if q == 1 else [sums[0][q], sums[1][q]]

    def stacked(parts):
        return jnp.stack(parts).reshape(4, 4, 2, inputs.shape[0], units)

    second_core = jnp.logical_not(first_core)
    own, other = reduce_rows(
        stacked(sums[0]), stacked(sums[1]), at_row, (second_core, first_core)
    )
    pre, grad_act = jnp.where(first_core, own, other), jnp.where(first_core, other, own)
    act_own, grad_pre_own = gelu_parts(
        pre * (1 / PRE_SCALE), turn(grad_act) * (1 / GRAD_SCALE)
    )

    half = width // 2
    give_weight = lax.dynamic_slice_in_dim(up, (1 - core) * half, half, 0)
    keep_weight = lax.dynamic_slice_in_dim(up, core * half, half, 0)
    grad_pre, act = gather_rows(
        grad_pre_own, act_own, at_row, (give_weight, keep_weight)
    )
    grad_pre = grad_pre.reshape(tokens, units)
    near = [jnp.where(first_core, p, o) for p, o in zip(pieces, others)]
    far = [jnp.where(first_core, o, p) for p, o in zip(pieces, others)]
    all_inputs, all_grads = jnp.concatenate(near, axis=0), jnp.concatenate(far, axis=0)

    act = jnp.swapaxes(act, 0, 1).reshape(tokens, units)

    def weight_gradients(sent):
        grad_up = contract_first(behind(all_inputs, sent), grad_pre)
        grad_down = contract_first(act, behind(all_grads, sent))
        return grad_up.astype(jnp.bfloat16), grad_down.astype(jnp.bfloat16)

    grad_inputs, (grad_up, grad_down) = scatter_tokens(
        grad_pre, keep_weight, give_weight, core, weight_gradients
    )
    return (grad_inputs, grad_up, grad_down)


def solution(mesh):
    in_specs = (P("col", "row"), P("col", "row"), P("row", "col"), P("col", "row"))
    out_specs = (P("col", "row"), P("row", "col"), P("col", "row"))
    return jax.shard_map(
        on_device, mesh=mesh, in_specs=in_specs, out_specs=out_specs, check_vma=False
    )
```

```python
import jax
import jax.numpy as jnp
from jax import lax
from jax.experimental import pallas as pl
from jax.experimental.pallas import tpu as pltpu
from jax.sharding import PartitionSpec as P

PRE_SCALE = 32.0
GRAD_SCALE = 128.0
SENT = jnp.float16


def gelu_parts(pre, grad_act):
    act, pull = jax.vjp(lambda value: jax.nn.gelu(value, approximate=True), pre)
    return (act.astype(jnp.bfloat16), pull(grad_act)[0].astype(jnp.bfloat16))


def contract_first(left, right):
    return lax.dot_general(
        left, right, (((0,), (0,)), ((), ())), preferred_element_type=jnp.float32
    )


def contract_last(left, right):
    return lax.dot_general(
        left, right, (((1,), (1,)), ((), ())), preferred_element_type=jnp.float32
    )


ALONG = (1, -1, 2)


def col_pairs(to):
    pairs = []
    for x in range(4):
        for y in range(4):
            for c in range(2):
                tx, ty, tc = to(x, y, c)
                there = ((tx % 4) * 4 + ty % 4) * 2 + tc
                pairs.append(((x * 4 + y) * 2 + c, there))
    return pairs


def swap(value):
    return lax.ppermute(value, "col", col_pairs(lambda x, y, c: (x, y, 1 - c)))


def move(value, axis_of_core, step):
    def to(x, y, c):
        return (x + step, y, c) if axis_of_core[c] == "x" else (x, y + step, c)

    return lax.ppermute(value, "col", col_pairs(to))


def move_row(value, step):
    return lax.ppermute(value, "row", [(i, (i + step) % 8) for i in range(8)])


def nothing(*refs):
    pass


def behind(value, *earlier):
    anywhere = pl.BlockSpec(memory_space=pl.ANY)
    return pl.pallas_call(
        nothing,
        out_shape=jax.ShapeDtypeStruct(value.shape, value.dtype),
        in_specs=[anywhere] * (1 + len(earlier)),
        out_specs=anywhere,
        input_output_aliases={0: 0},
        compiler_params=pltpu.CompilerParams(vmem_limit_bytes=128 * 1024),
        cost_estimate=pl.CostEstimate(flops=0, bytes_accessed=0, transcendentals=0),
    )(value, *earlier)


def gather_tokens(pair):
    line = jnp.concatenate([pair] + [move(pair, "xy", step) for step in ALONG], axis=0)
    return [line] + [move(line, "yx", step) for step in ALONG]


def block_start(index, turned):
    index = lax.rem(index + 8, 8)
    y, x = index // 4 * 2, index // 2 % 2 * 2
    zero = jnp.zeros_like(index)
    first, second = jnp.where(turned, x, y), jnp.where(turned, y, x)
    return first, second, index % 2, zero, zero


def block_of(value, index, turned):
    rows, width = value.shape[3:]
    start = block_start(index, turned)
    return lax.dynamic_slice(value, start, (2, 2, 1, rows, width)).reshape(4 * rows, width)


def reduce_rows(first, second, at_row, turned):
    arrays, hops = (first, second), ({-1: 4, 1: 3}, {1: 4, -1: 3})
    running, sent = ({}, {}), second
    for s in range(4):
        for hop_count in (4, 3):
            for a in range(2):
                step = next(d for d in hops[a] if hops[a][d] == hop_count)
                left = hop_count - s
                if left < 1:
                    continue
                term = block_of(arrays[a], at_row + step * left, turned[a])
                if s:
                    term = running[a][step] + term
                sent = behind(term, sent)
                running[a][step] = move_row(sent.astype(SENT), step).astype(jnp.float32)
    return tuple(
        block_of(arrays[a], at_row, turned[a]) + running[a][1] + running[a][-1]
        for a in range(2)
    )


def turn(value):
    rows, width = value.shape
    square = value.reshape(2, 2, rows // 4, width)
    return jnp.swapaxes(square, 0, 1).reshape(rows, width)


def gather_rows(first, second, at_row, ready):
    rows, width = first.shape
    hops = ({1: 4, -1: 3}, {-1: 4, 1: 3})

    def put(whole, block, index):
        start = block_start(index, False)
        return lax.dynamic_update_slice(whole, block.reshape(2, 2, 1, rows // 4, width), start)

    empty = jnp.zeros((4, 4, 2, rows // 4, width), first.dtype)
    whole = [put(empty, first, at_row), put(empty, second, at_row)]
    moving, sent = ({1: first, -1: first}, {1: second, -1: second}), None
    for s in range(4):
        for a in range(2):
            for step in hops[a]:
                if s >= hops[a][step]:
                    continue
                if s:
                    sent = behind(moving[a][step], sent, *ready)
                    ready = ()
                    whole[a] = put(whole[a], sent, at_row - step * s)
                else:
                    sent = moving[a][step]
                moving[a][step] = move_row(sent, step)
    for a in range(2):
        for step, last in hops[a].items():
            whole[a] = put(whole[a], moving[a][step], at_row - step * last)
    return whole


def scatter_tokens(grad_pre, keep_weight, give_weight, core, meanwhile):
    first_core = core == 0
    straight = grad_pre.reshape(4, -1, grad_pre.shape[1])
    turned = grad_pre.reshape(4, 4, -1, grad_pre.shape[1])
    turned = jnp.swapaxes(turned, 0, 1).reshape(straight.shape)
    mine = jnp.where(first_core, straight, turned)
    theirs = jnp.where(first_core, turned, straight)
    parts, sent = {}, None
    given = None
    for q in (3, 1, 2, 0):
        rows = theirs[q] if given is None else behind(theirs[q], given)
        given = (contract_last(rows, give_weight) * (1 / PRE_SCALE)).astype(jnp.bfloat16)
        kept = contract_last(mine[q], keep_weight) * (1 / PRE_SCALE)
        parts[q] = kept + swap(given).astype(jnp.float32)
    line = parts[0]
    for q, step in ((3, 2), (1, -1), (2, 1)):
        part = parts[q].astype(jnp.bfloat16)
        sent = part if sent is None else behind(part, sent)
        line = line + move(sent, "yx", step).astype(jnp.float32)
    done = meanwhile(sent)
    line = behind(line, *done).reshape(4, -1, line.shape[1])
    own = line[0]
    for p, step in ((3, 2), (1, -1), (2, 1)):
        part = move(line[p].astype(jnp.bfloat16), "xy", step)
        own = own + part.astype(jnp.float32)
    own = own.astype(jnp.bfloat16)
    rows, width = own.shape[0] // 2, own.shape[1]
    kept = lax.dynamic_slice(own, (core * rows, 0), (rows, width))
    other = swap(lax.dynamic_slice(own, ((1 - core) * rows, 0), (rows, width)))
    whole = jnp.where(
        first_core,
        jnp.concatenate([kept, other], axis=1),
        jnp.concatenate([other, kept], axis=1),
    )
    return whole, done


def on_device(inputs, grad_output, up_weight, down_weight):
    at_row = lax.axis_index("row")
    core = lax.rem(lax.axis_index("col"), 2)
    first_core = core == 0
    tokens, width = 32 * inputs.shape[0], inputs.shape[1]

    pair = jnp.where(
        first_core,
        jnp.concatenate([inputs, swap(inputs)], axis=0),
        jnp.concatenate([swap(grad_output), grad_output], axis=0),
    )
    pieces = gather_tokens(pair)

    scales = jnp.array([PRE_SCALE, GRAD_SCALE], jnp.float32).astype(jnp.bfloat16)
    scales = behind(jnp.broadcast_to(scales[:, None], (2, 128)), pieces[0])
    up, down = up_weight * scales[0, 0], down_weight.T * scales[1, 0]
    weights = jnp.where(first_core, up, down), jnp.where(first_core, down, up)
    units = up.shape[1]
    sums, others, earlier = ([None] * 4, [None] * 4), [None] * 4, []
    for q in (0, 3, 1, 2):
        if q:
            pieces[q] = behind(pieces[q], *earlier)
        others[q] = swap(pieces[q])
        for a, piece in enumerate((pieces[q], others[q])):
            sums[a][q] = jnp.dot(piece, weights[a], preferred_element_type=jnp.float32)
        earlier = [pieces[1]] if q == 1 else [sums[0][q], sums[1][q]]

    def stacked(parts):
        return jnp.stack(parts).reshape(4, 4, 2, inputs.shape[0], units)

    second_core = jnp.logical_not(first_core)
    own, other = reduce_rows(
        stacked(sums[0]), stacked(sums[1]), at_row, (second_core, first_core)
    )
    pre, grad_act = jnp.where(first_core, own, other), jnp.where(first_core, other, own)
    act_own, grad_pre_own = gelu_parts(
        pre * (1 / PRE_SCALE), turn(grad_act) * (1 / GRAD_SCALE)
    )

    half = width // 2
    give_weight = lax.dynamic_slice_in_dim(up, (1 - core) * half, half, 0)
    keep_weight = lax.dynamic_slice_in_dim(up, core * half, half, 0)
    grad_pre, act = gather_rows(
        grad_pre_own, act_own, at_row, (give_weight, keep_weight)
    )
    grad_pre = grad_pre.reshape(tokens, units)
    near = [jnp.where(first_core, p, o) for p, o in zip(pieces, others)]
    far = [jnp.where(first_core, o, p) for p, o in zip(pieces, others)]
    all_inputs, all_grads = jnp.concatenate(near, axis=0), jnp.concatenate(far, axis=0)

    act = jnp.swapaxes(act, 0, 1).reshape(tokens, units)

    def weight_gradients(sent):
        grad_up = contract_first(behind(all_inputs, sent), grad_pre)
        grad_down = contract_first(act, behind(all_grads, sent))
        return grad_up.astype(jnp.bfloat16), grad_down.astype(jnp.bfloat16)

    grad_inputs, (grad_up, grad_down) = scatter_tokens(
        grad_pre, keep_weight, give_weight, core, weight_gradients
    )
    return (grad_inputs, grad_up, grad_down)


def solution(mesh):
    in_specs = (P("col", "row"), P("col", "row"), P("row", "col"), P("col", "row"))
    out_specs = (P("col", "row"), P("row", "col"), P("col", "row"))
    return jax.shard_map(
        on_device, mesh=mesh, in_specs=in_specs, out_specs=out_specs, check_vma=False
    )
```
